32 devices in a mesh: seq: 8 (over y, x, core), exp: 4 (over z).
Axes of the slice: x: 2, y: 2, z: 4, core: 2. Of those that a mesh axis runs over, the one named last changes fastest.
Arguments:
- tokens: bfloat16 [2, 4096, 1024], P(None, 'seq'), may hold values from -48 to 48
- router: bfloat16 [1024, 512], P(None, 'exp'), may hold values from -4 to 4
- w_in: bfloat16 [32, 1024, 2048], P(('exp', 'seq')), may hold values from -0.1875 to 0.1875
- w_out: bfloat16 [32, 2048, 1024], P(('exp', 'seq')), may hold values from -0.125 to 0.125
Outputs:
- mixed: bfloat16 [2, 4096, 1024], P(None, ('seq', 'exp'))
The draws below stay inside these ranges and needn't reach their ends.
All inputs are finite; a program needn't handle non-finite values.
Results may differ from the reference program's by a relative error of at most 0.015.
Values may be sent and summed in bfloat16 or wider, within the bound.
A program may use at most 64 MiB of HBM per device.

```python
import jax
import jax.numpy as jnp
from jax import lax

D = 1024
FF = 2048
EXP_DEV = 8
SLOTS = 16
SEQS = 2
EXPERTS = 32
LEN = 4096
FF_SPLIT = 1
N_SEQ = 8


def draw_tokens(key, part):
    noise_key = jax.random.fold_in(jax.random.fold_in(key, 1), 0)
    base_noise = jnp.clip(jax.random.normal(noise_key, (SEQS, LEN, D), jnp.float32), -6.0, 6.0)
    position = jnp.arange(LEN, dtype=jnp.float32) / max(LEN - 1, 1)
    ramp_scale = 0.85 + 0.5 * position
    values = base_noise * ramp_scale[None, :, None]
    return values.astype(jnp.bfloat16)


def draw_router(key, part):
    noise_key = jax.random.fold_in(jax.random.fold_in(key, 2), 0)
    base_noise = jnp.clip(jax.random.normal(noise_key, (D, EXPERTS * SLOTS), jnp.float32), -6.0, 6.0)
    values = base_noise * (2.0 / D) ** 0.5
    return values.astype(jnp.bfloat16)


def level_of(stream_key, extent, pieces, smallest, high):
    gain = 1.0
    for axis_at, shards_of in pieces:
        heights = jax.random.uniform(jax.random.fold_in(jax.random.fold_in(stream_key, 6), axis_at), (shards_of,), jnp.float32, smallest / len(pieces), high / len(pieces))
        gain = gain * jnp.repeat(jnp.exp(heights), extent[axis_at] // shards_of).reshape((-1,) + (1,) * (len(extent) - 1 - axis_at))
    return gain


def centred(own_key, extent, spread, bound, pieces=(), kind=jnp.bfloat16):
    array = jax.random.normal(own_key, extent, jnp.float32) * spread
    if len(pieces) > 0:
        array = level_of(own_key, extent, pieces, -0.22, 0.18) * array
    return jnp.clip(array, min=-bound, max=bound).astype(kind)


def setup_inputs(seed: int = 0) -> dict:
    seeds = jax.random.split(jax.random.key(seed), 5)
    return {
        "tokens": draw_tokens(jax.random.fold_in(seeds[4], 71), 0),
        "router": draw_router(jax.random.fold_in(seeds[4], 71), 0),
        "w_in": centred(seeds[2], (EXPERTS * FF_SPLIT, D, FF // FF_SPLIT), D ** -0.5, 0.1875, ((0, 32),)),
        "w_out": centred(seeds[3], (EXPERTS * FF_SPLIT, FF // FF_SPLIT, D), FF ** -0.5, 0.125, ((0, 32),)),
    }


def reference(tokens, router, w_in, w_out):
    router_logits = jnp.einsum("bnq,qt->bnt", tokens.astype(jnp.float32), router.astype(jnp.float32))
    dispatch_weights = jax.nn.softmax(router_logits, axis=1).astype(jnp.bfloat16)
    slot_input_rows = jnp.einsum("mja,mjo->mao", dispatch_weights.astype(jnp.float32), tokens.astype(jnp.float32)).astype(jnp.bfloat16)
    split_count = N_SEQ // EXP_DEV
    piece_width = FF // split_count
    first_stack = w_in.reshape(EXPERTS, split_count, D, piece_width)
    second_stack = w_out.reshape(EXPERTS, split_count, piece_width, D)
    grouped_inputs = slot_input_rows.reshape(SEQS, EXPERTS, SLOTS, D)

    def apply_expert_network(expert_index):
        first_full = jnp.transpose(first_stack[expert_index], (1, 0, 2)).reshape(D, FF)
        second_full = second_stack[expert_index].reshape(FF, D)
        expert_input = grouped_inputs[:, expert_index].reshape(SEQS * SLOTS, D)
        pre_active = jnp.dot(expert_input, first_full, preferred_element_type=jnp.float32)
        hidden = jax.nn.gelu(pre_active, approximate=True).astype(jnp.bfloat16)
        result = jnp.dot(hidden, second_full, preferred_element_type=jnp.float32).astype(jnp.bfloat16)
        return result.reshape(SEQS, SLOTS, D)

    per_expert = lax.map(apply_expert_network, jnp.arange(EXPERTS, dtype=jnp.int32))
    slot_output_rows = jnp.transpose(per_expert, (1, 0, 2, 3)).reshape(SEQS, EXPERTS * SLOTS, D)
    combine_weights = jax.nn.softmax(router_logits, axis=2).astype(jnp.bfloat16)
    mixed = jnp.einsum("ptx,pxg->ptg", combine_weights.astype(jnp.float32), slot_output_rows.astype(jnp.float32))
    return mixed.astype(jnp.bfloat16)
```

```python
import functools

import jax
import jax.numpy as jnp
from jax import lax
from jax.experimental import pallas as pl
from jax.experimental.pallas import tpu as pltpu
from jax.sharding import PartitionSpec as P

SLOTS = 16
MESH = pl.DeviceIdType.MESH
F32 = jnp.float32
BF16 = jnp.bfloat16


def flip(index, mask):
    bit = 1
    while bit <= mask:
        if mask & bit:
            index = index + bit - 2 * bit * ((index // bit) % 2)
        bit *= 2
    return index


def partner(index, step, count):
    if count & (count - 1) == 0:
        return flip(index, step)
    return (index + step) % count


def layer(
    n_seq, n_exp,
    tokens_ref, router_ref, w_in_ref, w_out_ref, mixed_ref,
    tok, routers, w1, w2, psend, precv, ssend, srecv, coef, x_ref, pout, xrecv, slots, comb, inv,
    load_sem, rz_send, rz_recv, rs_send, rs_recv, p_send, p_recv, s_send, s_recv,
    q_send, q_recv, z_send, z_recv, c_send, c_recv, b_send, b_recv,
):
    seqs, length, width = tok.shape
    cols = router_ref.shape[1]
    hidden = w1.shape[1]
    experts = cols // SLOTS
    split = n_seq // experts
    chips = n_seq // 2
    rows = length // n_exp
    half = width // 2

    me_s = lax.axis_index("seq")
    me_e = lax.axis_index("exp")
    core = me_s % 2
    chip = me_s // 2
    sib = me_s + 1 - 2 * core
    own = me_s // split
    me_q = me_s % split

    loads = [
        pltpu.make_async_copy(router_ref, routers.at[me_e], load_sem.at[0]),
        pltpu.make_async_copy(tokens_ref, tok, load_sem.at[1]),
        pltpu.make_async_copy(w_in_ref.at[0], w1, load_sem.at[2]),
        pltpu.make_async_copy(w_out_ref.at[0], w2, load_sem.at[3]),
    ]
    for load in loads:
        load.start()

    barrier = pltpu.get_barrier_semaphore()
    for k in range(1, n_seq):
        pl.semaphore_signal(barrier, inc=1, device_id=(partner(me_s, k, n_seq), me_e), device_id_type=MESH)
    for k in range(1, n_exp):
        pl.semaphore_signal(barrier, inc=1, device_id=(me_s, partner(me_e, k, n_exp)), device_id_type=MESH)
    pl.semaphore_wait(barrier, n_seq + n_exp - 2)

    def remote(src, dst, send, recv, seq, exp):
        return pltpu.make_async_remote_copy(
            src_ref=src, dst_ref=dst, send_sem=send, recv_sem=recv,
            device_id=(seq, exp), device_id_type=MESH,
        )

    started = []

    def router_half(owner, which):
        return routers.at[owner, pl.ds(pl.multiple_of(which * half, half), half), :]

    loads[0].wait()
    for k in range(1, n_exp):
        other = partner(me_e, k, n_exp)
        piece = router_half(me_e, core)
        copy = remote(piece, piece, rz_send.at[k], rz_recv.at[k], me_s, other)
        copy.start()
        started.append(copy)

    loads[1].wait()
    ssend[...] = jnp.zeros_like(ssend)
    for s in range(seqs):
        score = jnp.dot(tok[s], routers[me_e], preferred_element_type=F32)
        top = jnp.max(score, axis=0, keepdims=True)
        weight = jnp.exp(score - top)
        ssend[s : s + 1, :] = top
        ssend[seqs + s : seqs + s + 1, :] = jnp.sum(weight, axis=0, keepdims=True)
        psend[s] = jnp.dot(weight.T.astype(BF16), tok[s], preferred_element_type=F32).astype(BF16)

    def slot_rows(expert):
        return pl.ds(pl.multiple_of(expert * SLOTS, SLOTS), SLOTS)

    for k in range(1, n_seq):
        other = partner(me_s, k, n_seq)
        for copy in (
            remote(ssend, srecv.at[me_s], s_send.at[k], s_recv.at[k], other, me_e),
            remote(psend.at[:, slot_rows(other // split), :], precv.at[me_s], p_send.at[k], p_recv.at[k], other, me_e),
        ):
            copy.start()
            started.append(copy)
    srecv[me_s] = ssend[...]
    precv[me_s] = psend[:, slot_rows(own), :]

    for k in range(1, n_exp):
        other = partner(me_e, k, n_exp)
        piece = router_half(other, core)
        remote(piece, piece, rz_send.at[k], rz_recv.at[k], me_s, other).wait_recv()
        copy = remote(piece, piece, rs_send.at[k], rs_recv.at[k], sib, me_e)
        copy.start()
        started.append(copy)
    for k in range(1, n_exp):
        piece = router_half(partner(me_e, k, n_exp), 1 - core)
        remote(piece, piece, rs_send.at[k], rs_recv.at[k], sib, me_e).wait_recv()
    for s in range(seqs):
        mine = tok[s, pl.ds(pl.multiple_of(me_e * rows, rows), rows), :]
        score = jnp.concatenate(
            [jnp.dot(mine, routers[e], preferred_element_type=F32) for e in range(n_exp)], axis=1
        )
        weight = jnp.exp(score - jnp.max(score, axis=1, keepdims=True))
        inv[s] = jnp.broadcast_to(1.0 / jnp.sum(weight, axis=1, keepdims=True), (rows, 128))
        comb[s] = weight.astype(BF16)

    for k in range(1, n_seq):
        other = partner(me_s, k, n_seq)
        remote(ssend, srecv.at[other], s_send.at[k], s_recv.at[k], other, me_e).wait_recv()
    parts = []
    for s in range(seqs):
        top = srecv[:, s, :]
        scale = jnp.exp(top - jnp.max(top, axis=0, keepdims=True))
        total = jnp.sum(scale * srecv[:, seqs + s, :], axis=0, keepdims=True)
        parts.append(scale / total)
    fill = coef.shape[1] - seqs * n_seq
    if fill:
        parts.append(jnp.zeros((fill, cols), F32))
    coef[...] = jnp.concatenate(parts, axis=0).T
    factor = coef[slot_rows(own), :]
    for k in range(1, n_seq):
        other = partner(me_s, k, n_seq)
        remote(psend.at[:, slot_rows(own), :], precv.at[other], p_send.at[k], p_recv.at[k], other, me_e).wait_recv()
    for s in range(seqs):
        total = jnp.zeros((SLOTS, width), F32)
        for i in range(n_seq):
            at = s * n_seq + i
            total = total + factor[:, at : at + 1] * precv[i, s].astype(F32)
        x_ref[s * SLOTS : (s + 1) * SLOTS, :] = total.astype(BF16)

    loads[2].wait()
    loads[3].wait()
    x = x_ref[...]
    block = min(512, hidden)
    result = jnp.zeros((seqs * SLOTS, width), F32)
    for at in range(0, hidden, block):
        pre = jnp.dot(x, w1[:, at : at + block], preferred_element_type=F32)
        act = jax.nn.gelu(pre, approximate=True).astype(BF16)
        result = result + jnp.dot(act, w2[at : at + block, :], preferred_element_type=F32)

    def place(exp, seq):
        return slots.at[seq % split, :, slot_rows(exp * experts + seq // split), :]

    part = width // split
    if split == 1:
        slots[0, :, slot_rows(me_e * experts + own), :] = result.reshape(seqs, SLOTS, width).astype(BF16)
    else:
        for q in range(split):
            pout[q] = result[:, q * part : (q + 1) * part].reshape(seqs, SLOTS, part).astype(BF16)
        for k in range(1, split):
            other = (me_q + k) % split
            copy = remote(pout.at[other], xrecv.at[k], q_send.at[k], q_recv.at[k], me_s - me_q + other, me_e)
            copy.start()
            started.append(copy)
        total = pout[me_q].astype(F32)
        for k in range(1, split):
            remote(pout.at[me_q], xrecv.at[k], q_send.at[k], q_recv.at[k], me_s, me_e).wait_recv()
            total = total + xrecv[k].astype(F32)
        slots[me_q, :, slot_rows(me_e * experts + own), :] = total.astype(BF16)

    for k in range(1, n_exp):
        piece = place(me_e, me_s)
        copy = remote(piece, piece, z_send.at[k], z_recv.at[k], me_s, partner(me_e, k, n_exp))
        copy.start()
        started.append(copy)
    for j in range(n_exp):
        exp = partner(me_e, j, n_exp) if j else me_e
        piece = place(exp, me_s)
        if j:
            remote(piece, piece, z_send.at[j], z_recv.at[j], me_s, exp).wait_recv()
        for k in range(1, chips):
            copy = remote(piece, piece, c_send.at[j, k], c_recv.at[j, k], partner(chip, k, chips) * 2 + core, me_e)
            copy.start()
            started.append(copy)
        copy = remote(piece, piece, b_send.at[j, 0], b_recv.at[j, 0], sib, me_e)
        copy.start()
        started.append(copy)
    for j in range(n_exp):
        exp = partner(me_e, j, n_exp) if j else me_e
        for k in range(1, chips):
            seq = partner(chip, k, chips) * 2 + core
            piece = place(exp, seq)
            remote(piece, piece, c_send.at[j, k], c_recv.at[j, k], seq, me_e).wait_recv()
            copy = remote(piece, piece, b_send.at[j, k], b_recv.at[j, k], sib, me_e)
            copy.start()
            started.append(copy)
    for j in range(n_exp):
        exp = partner(me_e, j, n_exp) if j else me_e
        for k in range(chips):
            seq = (partner(chip, k, chips) if k else chip) * 2 + 1 - core
            piece = place(exp, seq)
            remote(piece, piece, b_send.at[j, k], b_recv.at[j, k], sib, me_e).wait_recv()

    for s in range(seqs):
        scale = inv[s][:, 0:1]
        for q in range(split):
            mix = jnp.dot(comb[s], slots[q, s], preferred_element_type=F32) * scale
            mixed_ref[s, :, q * part : (q + 1) * part] = mix.astype(BF16)

    for copy in started:
        copy.wait_send()


def shards(n_seq, n_exp, tokens, router, w_in, w_out):
    seqs, length, width = tokens.shape
    cols = router.shape[1]
    hidden = w_in.shape[2]
    experts = cols // SLOTS
    split = n_seq // experts
    chips = n_seq // 2
    rows = length // n_exp
    part = width // split
    stat_rows = -(-2 * seqs // 8) * 8
    lanes = -(-seqs * n_seq // 128) * 128
    dma = pltpu.SemaphoreType.DMA
    return pl.pallas_call(
        functools.partial(layer, n_seq, n_exp),
        out_shape=jax.ShapeDtypeStruct((seqs, rows, width), BF16),
        in_specs=[pl.BlockSpec(memory_space=pl.ANY)] * 4,
        out_specs=pl.BlockSpec(memory_space=pltpu.VMEM),
        scratch_shapes=[
            pltpu.VMEM((seqs, length, width), BF16),
            pltpu.VMEM((n_exp, width, cols), BF16),
            pltpu.VMEM((width, hidden), BF16),
            pltpu.VMEM((hidden, width), BF16),
            pltpu.VMEM((seqs, cols, width), BF16),
            pltpu.VMEM((n_seq, seqs, SLOTS, width), BF16),
            pltpu.VMEM((stat_rows, cols), F32),
            pltpu.VMEM((n_seq, stat_rows, cols), F32),
            pltpu.VMEM((cols, lanes), F32),
            pltpu.VMEM((seqs * SLOTS, width), BF16),
            pltpu.VMEM((split, seqs, SLOTS, part), BF16),
            pltpu.VMEM((split, seqs, SLOTS, part), BF16),
            pltpu.VMEM((split, seqs, n_exp * cols, part), BF16),
            pltpu.VMEM((seqs, rows, n_exp * cols), BF16),
            pltpu.VMEM((seqs, rows, 128), F32),
            dma((4,)),
            dma((n_exp,)), dma((n_exp,)), dma((n_exp,)), dma((n_exp,)),
            dma((n_seq,)), dma((n_seq,)), dma((n_seq,)), dma((n_seq,)),
            dma((split,)), dma((split,)),
            dma((n_exp,)), dma((n_exp,)),
            dma((n_exp, chips)), dma((n_exp, chips)),
            dma((n_exp, chips)), dma((n_exp, chips)),
        ],
        compiler_params=pltpu.CompilerParams(
            collective_id=0, has_side_effects=True, vmem_limit_bytes=56 * 1024 * 1024
        ),
    )(tokens, router, w_in, w_out)


def solution(mesh):
    placed = (
        P(None, "seq", None),
        P(None, "exp"),
        P(("exp", "seq"), None, None),
        P(("exp", "seq"), None, None),
    )
    return jax.shard_map(
        functools.partial(shards, mesh.shape["seq"], mesh.shape["exp"]),
        mesh=mesh, in_specs=placed, out_specs=P(None, ("seq", "exp"), None), check_vma=False,
    )
```

```python
import functools

import jax
import jax.numpy as jnp
from jax import lax
from jax.experimental import pallas as pl
from jax.experimental.pallas import tpu as pltpu
from jax.sharding import PartitionSpec as P

SLOTS = 16
MESH = pl.DeviceIdType.MESH
F32 = jnp.float32
BF16 = jnp.bfloat16


def flip(index, mask):
    bit = 1
    while bit <= mask:
        if mask & bit:
            index = index + bit - 2 * bit * ((index // bit) % 2)
        bit *= 2
    return index


def partner(index, step, count):
    if count & (count - 1) == 0:
        return flip(index, step)
    return (index + step) % count


def grid_of(chips):
    cols = 1
    while cols * cols * 4 <= chips and chips % (cols * 2) == 0:
        cols *= 2
    return chips // cols, cols


def loop(start, stop, step):
    if stop - start <= 4:
        for j in range(start, stop):
            step(j)
    else:
        pl.loop(start, stop)(step)


def layer(
    n_seq, n_exp,
    tokens_ref, router_ref, w_in_ref, w_out_ref, mixed_ref,
    tok, routers, w1, w2, psend, precv, ssend, srecv, coef, x_ref, pout, xrecv, slots, comb, inv,
    load_sem, rz_send, rz_recv, rs_send, rs_recv, p_send, p_recv, s_send, s_recv,
    q_send, q_recv, z_send, z_recv, c_send, c_recv, d_send, d_recv, b_send, b_recv,
):
    seqs, length, width = tok.shape
    cols = router_ref.shape[1]
    hidden = w1.shape[1]
    experts = cols // SLOTS
    split = n_seq // experts
    chips = n_seq // 2
    rows = length // n_exp
    half = width // 2

    me_s = lax.axis_index("seq")
    me_e = lax.axis_index("exp")
    core = me_s % 2
    chip = me_s // 2
    sib = me_s + 1 - 2 * core
    own = me_s // split
    me_q = me_s % split

    loads = [
        pltpu.make_async_copy(router_ref, routers.at[me_e], load_sem.at[0]),
        pltpu.make_async_copy(tokens_ref, tok, load_sem.at[1]),
        pltpu.make_async_copy(w_in_ref.at[0], w1, load_sem.at[2]),
        pltpu.make_async_copy(w_out_ref.at[0], w2, load_sem.at[3]),
    ]
    loads[0].start()
    loads[1].start()

    barrier = pltpu.get_barrier_semaphore()
    for k in range(1, n_seq):
        pl.semaphore_signal(barrier, inc=1, device_id=(partner(me_s, k, n_seq), me_e), device_id_type=MESH)
    for k in range(1, n_exp):
        pl.semaphore_signal(barrier, inc=1, device_id=(me_s, partner(me_e, k, n_exp)), device_id_type=MESH)
    pl.semaphore_wait(barrier, n_seq + n_exp - 2)

    def remote(src, dst, send, recv, seq, exp):
        return pltpu.make_async_remote_copy(
            src_ref=src, dst_ref=dst, send_sem=send, recv_sem=recv,
            device_id=(seq, exp), device_id_type=MESH,
        )

    started = []

    def router_half(owner, which):
        return routers.at[owner, pl.ds(pl.multiple_of(which * half, half), half), :]

    loads[0].wait()
    for k in range(1, n_exp):
        other = partner(me_e, k, n_exp)
        piece = router_half(me_e, core)
        copy = remote(piece, piece, rz_send.at[k], rz_recv.at[k], me_s, other)
        copy.start()
        started.append(copy)

    loads[1].wait()
    loads[2].start()
    loads[3].start()
    ssend[...] = jnp.zeros_like(ssend)
    for s in range(seqs):
        score = jnp.dot(tok[s], routers[me_e], preferred_element_type=F32)
        top = jnp.max(score, axis=0, keepdims=True)
        weight = jnp.exp(score - top)
        ssend[s : s + 1, :] = top
        ssend[seqs + s : seqs + s + 1, :] = jnp.sum(weight, axis=0, keepdims=True)
        psend[s] = jnp.dot(weight.T.astype(BF16), tok[s], preferred_element_type=F32).astype(BF16)

    def slot_rows(expert):
        return pl.ds(pl.multiple_of(expert * SLOTS, SLOTS), SLOTS)

    for k in range(1, n_seq):
        other = partner(me_s, k, n_seq)
        for copy in (
            remote(ssend, srecv.at[me_s], s_send.at[k], s_recv.at[k], other, me_e),
            remote(psend.at[:, slot_rows(other // split), :], precv.at[me_s], p_send.at[k], p_recv.at[k], other, me_e),
        ):
            copy.start()
            started.append(copy)
    srecv[me_s] = ssend[...]
    precv[me_s] = psend[:, slot_rows(own), :]

    for k in range(1, n_seq):
        other = partner(me_s, k, n_seq)
        remote(ssend, srecv.at[other], s_send.at[k], s_recv.at[k], other, me_e).wait_recv()
    parts = []
    for s in range(seqs):
        top = srecv[:, s, :]
        scale = jnp.exp(top - jnp.max(top, axis=0, keepdims=True))
        total = jnp.sum(scale * srecv[:, seqs + s, :], axis=0, keepdims=True)
        parts.append(scale / total)
    fill = coef.shape[1] - seqs * n_seq
    if fill:
        parts.append(jnp.zeros((fill, cols), F32))
    coef[...] = jnp.concatenate(parts, axis=0).T
    factor = coef[slot_rows(own), :]
    for k in range(1, n_seq):
        other = partner(me_s, k, n_seq)
        remote(psend.at[:, slot_rows(own), :], precv.at[other], p_send.at[k], p_recv.at[k], other, me_e).wait_recv()
    for s in range(seqs):
        total = jnp.zeros((SLOTS, width), F32)
        for i in range(n_seq):
            at = s * n_seq + i
            total = total + factor[:, at : at + 1] * precv[i, s].astype(F32)
        x_ref[s * SLOTS : (s + 1) * SLOTS, :] = total.astype(BF16)

    for k in range(1, n_exp):
        other = partner(me_e, k, n_exp)
        piece = router_half(other, core)
        remote(piece, piece, rz_send.at[k], rz_recv.at[k], me_s, other).wait_recv()
        copy = remote(piece, piece, rs_send.at[k], rs_recv.at[k], sib, me_e)
        copy.start()
        started.append(copy)
    loads[2].wait()
    loads[3].wait()
    x = x_ref[...]
    block = min(512, hidden)
    result = jnp.zeros((seqs * SLOTS, width), F32)
    for at in range(0, hidden, block):
        pre = jnp.dot(x, w1[:, at : at + block], preferred_element_type=F32)
        act = jax.nn.gelu(pre, approximate=True).astype(BF16)
        result = result + jnp.dot(act, w2[at : at + block, :], preferred_element_type=F32)

    def place(exp, seq):
        return slots.at[seq % split, :, slot_rows(exp * experts + seq // split), :]

    part = width // split
    if split == 1:
        slots[0, :, slot_rows(me_e * experts + own), :] = result.reshape(seqs, SLOTS, width).astype(BF16)
    else:
        for q in range(split):
            pout[q] = result[:, q * part : (q + 1) * part].reshape(seqs, SLOTS, part).astype(BF16)
        for k in range(1, split):
            other = (me_q + k) % split
            copy = remote(pout.at[other], xrecv.at[k], q_send.at[k], q_recv.at[k], me_s - me_q + other, me_e)
            copy.start()
            started.append(copy)
        total = pout[me_q].astype(F32)
        for k in range(1, split):
            remote(pout.at[me_q], xrecv.at[k], q_send.at[k], q_recv.at[k], me_s, me_e).wait_recv()
            total = total + xrecv[k].astype(F32)
        slots[me_q, :, slot_rows(me_e * experts + own), :] = total.astype(BF16)

    grid_rows, grid_cols = grid_of(chips)
    my_row = chip // grid_cols
    my_col = chip % grid_cols

    def peer(axis, k):
        if axis == 0:
            return partner(my_row, k, grid_rows) * grid_cols + my_col
        return my_row * grid_cols + partner(my_col, k, grid_cols)

    def corner(k0, k1):
        return partner(my_row, k0, grid_rows) * grid_cols + partner(my_col, k1, grid_cols)

    sizes = (grid_rows, grid_cols)
    def one(exp, seq, s):
        return slots.at[seq % split, s, slot_rows(exp * experts + seq // split), :]

    far = (2 * me_e) // n_exp
    inner = 2 * (me_e + far * (n_exp - 1 - 2 * me_e))

    def nearest(j):
        outer = -((inner - j) // (2 * n_exp))
        sign = 2 * (j % 2) - 1
        exp = (1 - outer) * (me_e + sign * ((j + 1) // 2)) + outer * (j + far * (n_exp - 1 - 2 * j))
        return exp, outer * (2 * far - 1) - (1 - outer) * sign

    def along(exp, way):
        at, hops = (1 - way) // 2, way * (me_e - exp)
        piece = place(exp, me_s)
        return remote(piece, piece, z_send.at[at, hops], z_recv.at[at, hops + 1], me_s, me_e + way)

    def arrival(exp, way):
        at, hops = (1 - way) // 2, way * (me_e - exp)
        piece = place(exp, me_s)
        return remote(piece, piece, z_send.at[at, hops], z_recv.at[at, hops], me_s, me_e)

    def inside(at):
        return (at >= 0) & (at < n_exp)

    def direct(exp, s, axis, k):
        piece = one(exp, me_s, s)
        return remote(piece, piece, c_send.at[exp, s, axis, k], c_recv.at[exp, s, axis, k], peer(axis, k) * 2 + core, me_e)

    def direct_in(exp, s, axis, k):
        piece = one(exp, peer(axis, k) * 2 + core, s)
        return remote(piece, piece, c_send.at[exp, s, axis, k], c_recv.at[exp, s, axis, k], me_s, me_e)

    def turned(exp, s, k0, k1):
        first = s % 2
        piece = one(exp, peer(first, k0) * 2 + core, s)
        return remote(piece, piece, d_send.at[exp, s, k0, k1], d_recv.at[exp, s, k0, k1], peer(1 - first, k1) * 2 + core, me_e)

    def turned_in(exp, s, k0, k1):
        row, col = (k0, k1) if s % 2 == 0 else (k1, k0)
        piece = one(exp, corner(row, col) * 2 + core, s)
        return remote(piece, piece, d_send.at[exp, s, k0, k1], d_recv.at[exp, s, k0, k1], me_s, me_e)

    def to_sibling(exp, row, col):
        piece = place(exp, corner(row, col) * 2 + core)
        return remote(piece, piece, b_send.at[exp, row, col], b_recv.at[exp, row, col], sib, me_e)

    def from_sibling(exp, row, col):
        piece = place(exp, corner(row, col) * 2 + 1 - core)
        return remote(piece, piece, b_send.at[exp, row, col], b_recv.at[exp, row, col], sib, me_e)

    def spread(exp):
        for s in range(seqs):
            for axis in (s % 2, 1 - s % 2):
                for k in range(1, sizes[axis]):
                    direct(exp, s, axis, k).start()
        to_sibling(exp, 0, 0).start()

    def turn(exp):
        for s in range(seqs):
            first = s % 2
            for k0 in range(1, sizes[first]):
                direct_in(exp, s, first, k0).wait_recv()
                for k1 in range(1, sizes[1 - first]):
                    turned(exp, s, k0, k1).start()

    def share(exp):
        for s in range(seqs):
            second = 1 - s % 2
            for k in range(1, sizes[second]):
                direct_in(exp, s, second, k).wait_recv()
        for row in range(grid_rows):
            for col in range(grid_cols):
                if row == 0 or col == 0:
                    if row + col:
                        to_sibling(exp, row, col).start()
        for row in range(1, grid_rows):
            for col in range(1, grid_cols):
                for s in range(seqs):
                    turned_in(exp, s, *((row, col) if s % 2 == 0 else (col, row))).wait_recv()
                to_sibling(exp, row, col).start()

    def finish(exp):
        for row in range(grid_rows):
            for col in range(grid_cols):
                from_sibling(exp, row, col).wait_recv()
                to_sibling(exp, row, col).wait_send()
        for s in range(seqs):
            first = s % 2
            for axis in (0, 1):
                for k in range(1, sizes[axis]):
                    direct(exp, s, axis, k).wait_send()
            for k0 in range(1, sizes[first]):
                for k1 in range(1, sizes[1 - first]):
                    turned(exp, s, k0, k1).wait_send()

    for way in (1, -1):

        @pl.when(inside(me_e + way))
        def _():
            along(me_e, way).start()

    spread(me_e)
    for k in range(1, n_exp):
        piece = router_half(partner(me_e, k, n_exp), 1 - core)
        remote(piece, piece, rs_send.at[k], rs_recv.at[k], sib, me_e).wait_recv()
    for s in range(seqs):
        mine = tok[s, pl.ds(pl.multiple_of(me_e * rows, rows), rows), :]
        score = jnp.concatenate(
            [jnp.dot(mine, routers[e], preferred_element_type=F32) for e in range(n_exp)], axis=1
        )
        weight = jnp.exp(score - jnp.max(score, axis=1, keepdims=True))
        inv[s] = jnp.broadcast_to(1.0 / jnp.sum(weight, axis=1, keepdims=True), (rows, 128))
        comb[s] = weight.astype(BF16)


    def pass_on(j):
        exp, way = nearest(j)
        arrival(exp, way).wait_recv()

        @pl.when(inside(me_e + way))
        def _():
            along(exp, way).start()

        spread(exp)

    def step(j):
        pass_on(j)
        turn(nearest(j - 1)[0])

        if isinstance(j, int):
            if j >= 2:
                share(nearest(j - 2)[0])
        else:

            @pl.when(j >= 2)
            def _():
                share(nearest(j - 2)[0])

    loop(1, n_exp, step)
    turn(nearest(n_exp - 1)[0])
    loop(max(n_exp - 2, 0), n_exp, lambda j: share(nearest(j)[0]))

    for way in (1, -1):

        @pl.when(inside(me_e + way))
        def _():
            along(me_e, way).wait_send()

    def end(j):
        exp, way = nearest(j)

        @pl.when(inside(me_e + way))
        def _():
            along(exp, way).wait_send()

    loop(1, n_exp, end)
    loop(0, n_exp, finish)

    for s in range(seqs):
        scale = inv[s][:, 0:1]
        for q in range(split):
            mix = jnp.dot(comb[s], slots[q, s], preferred_element_type=F32) * scale
            mixed_ref[s, :, q * part : (q + 1) * part] = mix.astype(BF16)

    for copy in started:
        copy.wait_send()


def shards(n_seq, n_exp, tokens, router, w_in, w_out):
    seqs, length, width = tokens.shape
    cols = router.shape[1]
    hidden = w_in.shape[2]
    experts = cols // SLOTS
    split = n_seq // experts
    chips = n_seq // 2
    rows = length // n_exp
    part = width // split
    stat_rows = -(-2 * seqs // 8) * 8
    side = max(grid_of(chips))
    lanes = -(-seqs * n_seq // 128) * 128
    dma = pltpu.SemaphoreType.DMA
    return pl.pallas_call(
        functools.partial(layer, n_seq, n_exp),
        out_shape=jax.ShapeDtypeStruct((seqs, rows, width), BF16),
        in_specs=[pl.BlockSpec(memory_space=pl.ANY)] * 4,
        out_specs=pl.BlockSpec(memory_space=pltpu.VMEM),
        scratch_shapes=[
            pltpu.VMEM((seqs, length, width), BF16),
            pltpu.VMEM((n_exp, width, cols), BF16),
            pltpu.VMEM((width, hidden), BF16),
            pltpu.VMEM((hidden, width), BF16),
            pltpu.VMEM((seqs, cols, width), BF16),
            pltpu.VMEM((n_seq, seqs, SLOTS, width), BF16),
            pltpu.VMEM((stat_rows, cols), F32),
            pltpu.VMEM((n_seq, stat_rows, cols), F32),
            pltpu.VMEM((cols, lanes), F32),
            pltpu.VMEM((seqs * SLOTS, width), BF16),
            pltpu.VMEM((split, seqs, SLOTS, part), BF16),
            pltpu.VMEM((split, seqs, SLOTS, part), BF16),
            pltpu.VMEM((split, seqs, n_exp * cols, part), BF16),
            pltpu.VMEM((seqs, rows, n_exp * cols), BF16),
            pltpu.VMEM((seqs, rows, 128), F32),
            dma((4,)),
            dma((n_exp,)), dma((n_exp,)), dma((n_exp,)), dma((n_exp,)),
            dma((n_seq,)), dma((n_seq,)), dma((n_seq,)), dma((n_seq,)),
            dma((split,)), dma((split,)),
            dma((2, n_exp)), dma((2, n_exp)),
            dma((n_exp, seqs, 2, side)), dma((n_exp, seqs, 2, side)),
            dma((n_exp, seqs, side, side)), dma((n_exp, seqs, side, side)),
            dma((n_exp, *grid_of(chips))), dma((n_exp, *grid_of(chips))),
        ],
        compiler_params=pltpu.CompilerParams(
            collective_id=0, has_side_effects=True, vmem_limit_bytes=56 * 1024 * 1024
        ),
    )(tokens, router, w_in, w_out)


def solution(mesh):
    placed = (
        P(None, "seq", None),
        P(None, "exp"),
        P(("exp", "seq"), None, None),
        P(("exp", "seq"), None, None),
    )
    return jax.shard_map(
        functools.partial(shards, mesh.shape["seq"], mesh.shape["exp"]),
        mesh=mesh, in_specs=placed, out_specs=P(None, ("seq", "exp"), None), check_vma=False,
    )
```

```python
import functools

import jax
import jax.numpy as jnp
from jax import lax
from jax.experimental import pallas as pl
from jax.experimental.pallas import tpu as pltpu
from jax.sharding import PartitionSpec as P

SLOTS = 16
MESH = pl.DeviceIdType.MESH
F32 = jnp.float32
BF16 = jnp.bfloat16


def flip(index, mask):
    bit = 1
    while bit <= mask:
        if mask & bit:
            index = index + bit - 2 * bit * ((index // bit) % 2)
        bit *= 2
    return index


def partner(index, step, count):
    if count & (count - 1) == 0:
        return flip(index, step)
    return (index + step) % count


def layer(
    n_seq, n_exp,
    tokens_ref, router_ref, w_in_ref, w_out_ref, mixed_ref,
    tok, routers, w1, w2, psend, precv, ssend, srecv, coef, x_ref, pout, xrecv, slots, comb, inv, perm,
    load_sem, rz_send, rz_recv, rs_send, rs_recv, p_send, p_recv, s_send, s_recv,
    q_send, q_recv, z_send, z_recv, c_send, c_recv, b_send, b_recv,
):
    seqs, length, width = tok.shape
    cols = router_ref.shape[1]
    hidden = w1.shape[1]
    experts = cols // SLOTS
    split = n_seq // experts
    chips = n_seq // 2
    rows = length // n_exp
    half = width // 2

    me_s = lax.axis_index("seq")
    me_e = lax.axis_index("exp")
    core = me_s % 2
    chip = me_s // 2
    sib = me_s + 1 - 2 * core
    own = me_s // split
    me_q = me_s % split

    loads = [
        pltpu.make_async_copy(router_ref, routers.at[0], load_sem.at[0]),
        pltpu.make_async_copy(tokens_ref, tok, load_sem.at[1]),
        pltpu.make_async_copy(w_in_ref.at[0], w1, load_sem.at[2]),
        pltpu.make_async_copy(w_out_ref.at[0], w2, load_sem.at[3]),
    ]
    loads[0].start()
    loads[1].start()

    barrier = pltpu.get_barrier_semaphore()
    for k in range(1, n_seq):
        pl.semaphore_signal(barrier, inc=1, device_id=(partner(me_s, k, n_seq), me_e), device_id_type=MESH)
    for k in range(1, n_exp):
        pl.semaphore_signal(barrier, inc=1, device_id=(me_s, partner(me_e, k, n_exp)), device_id_type=MESH)
    pl.semaphore_wait(barrier, n_seq + n_exp - 2)

    def remote(src, dst, send, recv, seq, exp):
        return pltpu.make_async_remote_copy(
            src_ref=src, dst_ref=dst, send_sem=send, recv_sem=recv,
            device_id=(seq, exp), device_id_type=MESH,
        )

    started = []

    def router_half(k, which):
        return routers.at[k, pl.ds(pl.multiple_of(which * half, half), half), :]

    def router_over(k):
        return remote(
            router_half(0, core), router_half(k, core), rz_send.at[k], rz_recv.at[k], me_s, partner(me_e, k, n_exp)
        )

    def router_share(k, which):
        piece = router_half(k, which)
        return remote(piece, piece, rs_send.at[k], rs_recv.at[k], sib, me_e)

    loads[0].wait()
    for k in range(1, n_exp):
        router_over(k).start()
        started.append(router_over(k))

    if split == 1:
        count = n_exp * cols
        source = lax.broadcasted_iota(jnp.int32, (count, count), 0)
        target = lax.broadcasted_iota(jnp.int32, (count, count), 1)
        pair = 2 * SLOTS
        wanted = (
            (source // SLOTS) % 2 * (count // 2) + source // pair * SLOTS + source % SLOTS
        )
        perm[...] = (wanted == target).astype(F32).astype(BF16)

    loads[1].wait()
    loads[2].start()
    loads[3].start()
    ssend[...] = jnp.zeros_like(ssend)
    for s in range(seqs):
        score = jnp.dot(tok[s], routers[0], preferred_element_type=F32)
        top = jnp.max(score, axis=0, keepdims=True)
        weight = jnp.exp(score - top)
        ssend[s : s + 1, :] = top
        ssend[seqs + s : seqs + s + 1, :] = jnp.sum(weight, axis=0, keepdims=True)
        psend[s] = jnp.dot(weight.T.astype(BF16), tok[s], preferred_element_type=F32).astype(BF16)

    def slot_rows(expert):
        return pl.ds(pl.multiple_of(expert * SLOTS, SLOTS), SLOTS)

    for k in range(1, n_seq):
        other = partner(me_s, k, n_seq)
        for copy in (
            remote(ssend, srecv.at[me_s], s_send.at[k], s_recv.at[k], other, me_e),
            remote(psend.at[:, slot_rows(other // split), :], precv.at[me_s], p_send.at[k], p_recv.at[k], other, me_e),
        ):
            copy.start()
            started.append(copy)
    srecv[me_s] = ssend[...]
    precv[me_s] = psend[:, slot_rows(own), :]

    for k in range(1, n_seq):
        other = partner(me_s, k, n_seq)
        remote(ssend, srecv.at[other], s_send.at[k], s_recv.at[k], other, me_e).wait_recv()
    parts = []
    for s in range(seqs):
        top = srecv[:, s, :]
        scale = jnp.exp(top - jnp.max(top, axis=0, keepdims=True))
        total = jnp.sum(scale * srecv[:, seqs + s, :], axis=0, keepdims=True)
        parts.append(scale / total)
    fill = coef.shape[1] - seqs * n_seq
    if fill:
        parts.append(jnp.zeros((fill, cols), F32))
    coef[...] = jnp.concatenate(parts, axis=0).T
    factor = coef[slot_rows(own), :]
    for k in range(1, n_seq):
        other = partner(me_s, k, n_seq)
        remote(psend.at[:, slot_rows(own), :], precv.at[other], p_send.at[k], p_recv.at[k], other, me_e).wait_recv()
    for s in range(seqs):
        total = jnp.zeros((SLOTS, width), F32)
        for i in range(n_seq):
            at = s * n_seq + i
            total = total + factor[:, at : at + 1] * precv[i, s].astype(F32)
        x_ref[s * SLOTS : (s + 1) * SLOTS, :] = total.astype(BF16)

    loads[2].wait()
    loads[3].wait()
    x = x_ref[...]
    block = min(512, hidden)
    result = jnp.zeros((seqs * SLOTS, width), F32)
    for at in range(0, hidden, block):
        pre = jnp.dot(x, w1[:, at : at + block], preferred_element_type=F32)
        act = jax.nn.gelu(pre, approximate=True).astype(BF16)
        result = result + jnp.dot(act, w2[at : at + block, :], preferred_element_type=F32)

    def chip_rows(at):
        return pl.ds(pl.multiple_of(at * SLOTS, SLOTS), SLOTS)

    def place(first, last, at):
        return slots.at[core, :, first:last, chip_rows(at), :]

    part = width // split
    if split == 1:
        slots[core, :, 0, chip_rows(chip), :] = result.reshape(seqs, SLOTS, width).astype(BF16)
    else:
        for q in range(split):
            pout[q] = result[:, q * part : (q + 1) * part].reshape(seqs, SLOTS, part).astype(BF16)
        for k in range(1, split):
            other = (me_q + k) % split
            copy = remote(pout.at[other], xrecv.at[k], q_send.at[k], q_recv.at[k], me_s - me_q + other, me_e)
            copy.start()
            started.append(copy)
        total = pout[me_q].astype(F32)
        for k in range(1, split):
            remote(pout.at[me_q], xrecv.at[k], q_send.at[k], q_recv.at[k], me_s, me_e).wait_recv()
            total = total + xrecv[k].astype(F32)
        slots[core, :, 0, chip_rows(chip), :] = total.astype(BF16)

    groups = [(k, k + 1) for k in range(n_exp)]

    def over(k):
        return remote(
            place(0, 1, chip), place(k, k + 1, chip), z_send.at[k], z_recv.at[k], me_s, partner(me_e, k, n_exp)
        )

    def across(g, k):
        piece = place(*groups[g], chip)
        return remote(piece, piece, c_send.at[g, k], c_recv.at[g, k], partner(chip, k, chips) * 2 + core, me_e)

    def across_in(g, k):
        piece = place(*groups[g], partner(chip, k, chips))
        return remote(piece, piece, c_send.at[g, k], c_recv.at[g, k], me_s, me_e)

    def share(g, which):
        first, last = groups[g]
        piece = slots.at[which, :, first:last, :, :]
        return remote(piece, piece, b_send.at[g], b_recv.at[g], sib, me_e)

    for k in range(1, n_exp):
        over(k).start()
        started.append(over(k))
    for k in range(1, chips):
        across(0, k).start()
        started.append(across(0, k))
    for k in range(1, n_exp):
        router_over(k).wait_recv()
        router_share(k, core).start()
        started.append(router_share(k, core))
    for g in range(1, len(groups)):
        for k in range(*groups[g]):
            over(k).wait_recv()
        for k in range(1, chips):
            across(g, k).start()
            started.append(across(g, k))
    for k in range(1, n_exp):
        router_share(k, 1 - core).wait_recv()
    for s in range(seqs):
        mine = tok[s, pl.ds(pl.multiple_of(me_e * rows, rows), rows), :]
        score = jnp.concatenate(
            [jnp.dot(mine, routers[e], preferred_element_type=F32) for e in range(n_exp)], axis=1
        )
        weight = jnp.exp(score - jnp.max(score, axis=1, keepdims=True))
        inv[s] = jnp.broadcast_to(1.0 / jnp.sum(weight, axis=1, keepdims=True), (rows, 128))
        weight = weight.astype(BF16)
        if split == 1:
            weight = jnp.dot(weight, perm[...], preferred_element_type=F32).astype(BF16)
        comb[s] = weight


    for g in range(len(groups)):
        for k in range(1, chips):
            across_in(g, k).wait_recv()
        share(g, core).start()
        started.append(share(g, core))
    for g in range(len(groups)):
        share(g, 1 - core).wait_recv()

    for s in range(seqs):
        scale = inv[s][:, 0:1]
        if split == 1:
            side = n_exp * cols // 2
            mix = jnp.zeros((rows, width), F32)
            for c in range(2):
                mix = mix + jnp.dot(
                    comb[s, :, c * side : (c + 1) * side], slots[c, s].reshape(side, width),
                    preferred_element_type=F32,
                )
            mixed_ref[s] = (mix * scale).astype(BF16)
        else:
            sub = split // 2
            for q in range(split):
                piece = slots[q % 2, s].reshape(n_exp, chips // sub, sub, SLOTS, part)[:, :, q // 2]
                mix = jnp.dot(
                    comb[s], piece.reshape(n_exp * cols, part), preferred_element_type=F32
                )
                mixed_ref[s, :, q * part : (q + 1) * part] = (mix * scale).astype(BF16)

    for copy in started:
        copy.wait_send()


def shards(n_seq, n_exp, tokens, router, w_in, w_out):
    seqs, length, width = tokens.shape
    cols = router.shape[1]
    hidden = w_in.shape[2]
    experts = cols // SLOTS
    split = n_seq // experts
    chips = n_seq // 2
    rows = length // n_exp
    part = width // split
    stat_rows = -(-2 * seqs // 8) * 8
    lanes = -(-seqs * n_seq // 128) * 128
    dma = pltpu.SemaphoreType.DMA
    return pl.pallas_call(
        functools.partial(layer, n_seq, n_exp),
        out_shape=jax.ShapeDtypeStruct((seqs, rows, width), BF16),
        in_specs=[pl.BlockSpec(memory_space=pl.ANY)] * 4,
        out_specs=pl.BlockSpec(memory_space=pltpu.VMEM),
        scratch_shapes=[
            pltpu.VMEM((seqs, length, width), BF16),
            pltpu.VMEM((n_exp, width, cols), BF16),
            pltpu.VMEM((width, hidden), BF16),
            pltpu.VMEM((hidden, width), BF16),
            pltpu.VMEM((seqs, cols, width), BF16),
            pltpu.VMEM((n_seq, seqs, SLOTS, width), BF16),
            pltpu.VMEM((stat_rows, cols), F32),
            pltpu.VMEM((n_seq, stat_rows, cols), F32),
            pltpu.VMEM((cols, lanes), F32),
            pltpu.VMEM((seqs * SLOTS, width), BF16),
            pltpu.VMEM((split, seqs, SLOTS, part), BF16),
            pltpu.VMEM((split, seqs, SLOTS, part), BF16),
            pltpu.VMEM((2, seqs, n_exp, chips * SLOTS, part), BF16),
            pltpu.VMEM((seqs, rows, n_exp * cols), BF16),
            pltpu.VMEM((seqs, rows, 128), F32),
            pltpu.VMEM((n_exp * cols,) * 2 if split == 1 else (16, 128), BF16),
            dma((4,)),
            dma((n_exp,)), dma((n_exp,)), dma((n_exp,)), dma((n_exp,)),
            dma((n_seq,)), dma((n_seq,)), dma((n_seq,)), dma((n_seq,)),
            dma((split,)), dma((split,)),
            dma((n_exp,)), dma((n_exp,)),
            dma((n_exp, chips)), dma((n_exp, chips)),
            dma((n_exp,)), dma((n_exp,)),
        ],
        compiler_params=pltpu.CompilerParams(
            collective_id=0, has_side_effects=True, vmem_limit_bytes=56 * 1024 * 1024
        ),
    )(tokens, router, w_in, w_out)


def solution(mesh):
    placed = (
        P(None, "seq", None),
        P(None, "exp"),
        P(("exp", "seq"), None, None),
        P(("exp", "seq"), None, None),
    )
    return jax.shard_map(
        functools.partial(shards, mesh.shape["seq"], mesh.shape["exp"]),
        mesh=mesh, in_specs=placed, out_specs=P(None, ("seq", "exp"), None), check_vma=False,
    )
```

```python
import functools

import jax
import jax.numpy as jnp
from jax import lax
from jax.experimental import pallas as pl
from jax.experimental.pallas import tpu as pltpu
from jax.sharding import PartitionSpec as P

SLOTS = 16
MESH = pl.DeviceIdType.MESH
F32 = jnp.float32
BF16 = jnp.bfloat16


def flip(index, mask):
    bit = 1
    while bit <= mask:
        if mask & bit:
            index = index + bit - 2 * bit * ((index // bit) % 2)
        bit *= 2
    return index


def partner(index, step, count):
    if count & (count - 1) == 0:
        return flip(index, step)
    return (index + step) % count


def layer(
    n_seq, n_exp,
    tokens_ref, router_ref, w_in_ref, w_out_ref, mixed_ref,
    tok, routers, w1, w2, psend, precv, ssend, srecv, coef, x_ref, pout, xrecv, slots, comb, inv, perm,
    load_sem, rz_send, rz_recv, rs_send, rs_recv, p_send, p_recv, s_send, s_recv,
    q_send, q_recv, z_send, z_recv, c_send, c_recv, b_send, b_recv,
):
    seqs, length, width = tok.shape
    cols = router_ref.shape[1]
    hidden = w1.shape[1]
    experts = cols // SLOTS
    split = n_seq // experts
    chips = n_seq // 2
    rows = length // n_exp
    half = width // 2

    me_s = lax.axis_index("seq")
    me_e = lax.axis_index("exp")
    core = me_s % 2
    chip = me_s // 2
    sib = me_s + 1 - 2 * core
    own = me_s // split
    me_q = me_s % split

    loads = [
        pltpu.make_async_copy(router_ref, routers.at[0], load_sem.at[0]),
        pltpu.make_async_copy(tokens_ref, tok, load_sem.at[1]),
        pltpu.make_async_copy(w_in_ref.at[0], w1, load_sem.at[2]),
        pltpu.make_async_copy(w_out_ref.at[0], w2, load_sem.at[3]),
    ]
    loads[0].start()
    loads[1].start()

    barrier = pltpu.get_barrier_semaphore()
    for k in range(1, n_seq):
        pl.semaphore_signal(barrier, inc=1, device_id=(partner(me_s, k, n_seq), me_e), device_id_type=MESH)
    for k in range(1, n_exp):
        pl.semaphore_signal(barrier, inc=1, device_id=(me_s, partner(me_e, k, n_exp)), device_id_type=MESH)
    pl.semaphore_wait(barrier, n_seq + n_exp - 2)

    def remote(src, dst, send, recv, seq, exp):
        return pltpu.make_async_remote_copy(
            src_ref=src, dst_ref=dst, send_sem=send, recv_sem=recv,
            device_id=(seq, exp), device_id_type=MESH,
        )

    started = []

    def router_half(k, which):
        return routers.at[k, pl.ds(pl.multiple_of(which * half, half), half), :]

    def router_over(k):
        return remote(
            router_half(0, core), router_half(k, core), rz_send.at[k], rz_recv.at[k], me_s, partner(me_e, k, n_exp)
        )

    def router_share(k, which):
        piece = router_half(k, which)
        return remote(piece, piece, rs_send.at[k], rs_recv.at[k], sib, me_e)

    loads[0].wait()
    for k in range(1, n_exp):
        router_over(k).start()
        started.append(router_over(k))

    if split == 1:
        count = n_exp * cols
        source = lax.broadcasted_iota(jnp.int32, (count, count), 0)
        target = lax.broadcasted_iota(jnp.int32, (count, count), 1)
        pair = 2 * SLOTS
        wanted = (
            (source // SLOTS) % 2 * (count // 2) + source // pair * SLOTS + source % SLOTS
        )
        perm[...] = (wanted == target).astype(F32).astype(BF16)

    loads[1].wait()
    loads[2].start()
    loads[3].start()
    def slot_rows(expert):
        return pl.ds(pl.multiple_of(expert * SLOTS, SLOTS), SLOTS)

    def partial(s, k):
        other = partner(me_s, k, n_seq)
        return remote(
            psend.at[s, slot_rows(other // split), :], precv.at[me_s, s], p_send.at[s, k], p_recv.at[s, k], other, me_e
        )

    def partial_in(s, k):
        other = partner(me_s, k, n_seq)
        return remote(psend.at[s, slot_rows(own), :], precv.at[other, s], p_send.at[s, k], p_recv.at[s, k], other, me_e)

    order = [k for k in range(2, n_seq)] + [1]
    ssend[...] = jnp.zeros_like(ssend)
    for s in range(seqs):
        score = jnp.dot(tok[s], routers[0], preferred_element_type=F32)
        top = jnp.max(score, axis=0, keepdims=True)
        weight = jnp.exp(score - top)
        ssend[s : s + 1, :] = top
        ssend[seqs + s : seqs + s + 1, :] = jnp.sum(weight, axis=0, keepdims=True)
        psend[s] = jnp.dot(weight.T.astype(BF16), tok[s], preferred_element_type=F32).astype(BF16)
        for k in order:
            partial(s, k).start()
            started.append(partial(s, k))
    for k in order:
        copy = remote(ssend, srecv.at[me_s], s_send.at[k], s_recv.at[k], partner(me_s, k, n_seq), me_e)
        copy.start()
        started.append(copy)
    srecv[me_s] = ssend[...]
    precv[me_s] = psend[:, slot_rows(own), :]

    for k in range(1, n_seq):
        other = partner(me_s, k, n_seq)
        remote(ssend, srecv.at[other], s_send.at[k], s_recv.at[k], other, me_e).wait_recv()
    parts = []
    for s in range(seqs):
        top = srecv[:, s, :]
        scale = jnp.exp(top - jnp.max(top, axis=0, keepdims=True))
        total = jnp.sum(scale * srecv[:, seqs + s, :], axis=0, keepdims=True)
        parts.append(scale / total)
    fill = coef.shape[1] - seqs * n_seq
    if fill:
        parts.append(jnp.zeros((fill, cols), F32))
    coef[...] = jnp.concatenate(parts, axis=0).T
    factor = coef[slot_rows(own), :]
    for s in range(seqs):
        for k in range(1, n_seq):
            partial_in(s, k).wait_recv()
        total = jnp.zeros((SLOTS, width), F32)
        for i in range(n_seq):
            at = s * n_seq + i
            total = total + factor[:, at : at + 1] * precv[i, s].astype(F32)
        x_ref[s * SLOTS : (s + 1) * SLOTS, :] = total.astype(BF16)

    loads[2].wait()
    loads[3].wait()
    x = x_ref[...]
    block = min(512, hidden)
    result = jnp.zeros((seqs * SLOTS, width), F32)
    for at in range(0, hidden, block):
        pre = jnp.dot(x, w1[:, at : at + block], preferred_element_type=F32)
        act = jax.nn.gelu(pre, approximate=True).astype(BF16)
        result = result + jnp.dot(act, w2[at : at + block, :], preferred_element_type=F32)

    def chip_rows(at):
        return pl.ds(pl.multiple_of(at * SLOTS, SLOTS), SLOTS)

    def place(first, last, at):
        return slots.at[core, :, first:last, chip_rows(at), :]

    part = width // split
    if split == 1:
        slots[core, :, 0, chip_rows(chip), :] = result.reshape(seqs, SLOTS, width).astype(BF16)
    else:
        for q in range(split):
            pout[q] = result[:, q * part : (q + 1) * part].reshape(seqs, SLOTS, part).astype(BF16)
        for k in range(1, split):
            other = (me_q + k) % split
            copy = remote(pout.at[other], xrecv.at[k], q_send.at[k], q_recv.at[k], me_s - me_q + other, me_e)
            copy.start()
            started.append(copy)
        total = pout[me_q].astype(F32)
        for k in range(1, split):
            remote(pout.at[me_q], xrecv.at[k], q_send.at[k], q_recv.at[k], me_s, me_e).wait_recv()
            total = total + xrecv[k].astype(F32)
        slots[core, :, 0, chip_rows(chip), :] = total.astype(BF16)

    groups = [(k, k + 1) for k in range(n_exp)]

    bits = [1 << b for b in range(n_exp.bit_length() - 1)]

    def over(low, bit):
        k = low + bit
        return remote(
            place(low, low + 1, chip), place(k, k + 1, chip), z_send.at[k], z_recv.at[k],
            me_s, partner(me_e, bit, n_exp),
        )

    def across(g, k):
        piece = place(*groups[g], chip)
        return remote(piece, piece, c_send.at[g, k], c_recv.at[g, k], partner(chip, k, chips) * 2 + core, me_e)

    def across_in(g, k):
        piece = place(*groups[g], partner(chip, k, chips))
        return remote(piece, piece, c_send.at[g, k], c_recv.at[g, k], me_s, me_e)

    def share(g, which):
        first, last = groups[g]
        piece = slots.at[which, :, first:last, :, :]
        return remote(piece, piece, b_send.at[g], b_recv.at[g], sib, me_e)

    for bit in bits:
        over(0, bit).start()
        started.append(over(0, bit))
    for k in range(1, chips):
        across(0, k).start()
        started.append(across(0, k))
    for k in range(1, n_exp):
        router_over(k).wait_recv()
        router_share(k, core).start()
        started.append(router_share(k, core))
    for g in range(1, len(groups)):
        top = max(bit for bit in bits if bit <= g)
        over(g - top, top).wait_recv()
        for bit in bits:
            if bit > g:
                over(g, bit).start()
                started.append(over(g, bit))
        for k in range(1, chips):
            across(g, k).start()
            started.append(across(g, k))
    for k in range(1, n_exp):
        router_share(k, 1 - core).wait_recv()
    for s in range(seqs):
        mine = tok[s, pl.ds(pl.multiple_of(me_e * rows, rows), rows), :]
        score = jnp.concatenate(
            [jnp.dot(mine, routers[e], preferred_element_type=F32) for e in range(n_exp)], axis=1
        )
        weight = jnp.exp(score - jnp.max(score, axis=1, keepdims=True))
        inv[s] = jnp.broadcast_to(1.0 / jnp.sum(weight, axis=1, keepdims=True), (rows, 128))
        weight = weight.astype(BF16)
        if split == 1:
            weight = jnp.dot(weight, perm[...], preferred_element_type=F32).astype(BF16)
        comb[s] = weight


    for g in range(len(groups)):
        for k in range(1, chips):
            across_in(g, k).wait_recv()
        share(g, core).start()
        started.append(share(g, core))
    for g in range(len(groups)):
        share(g, 1 - core).wait_recv()

    for s in range(seqs):
        scale = inv[s][:, 0:1]
        if split == 1:
            side = n_exp * cols // 2
            mix = jnp.zeros((rows, width), F32)
            for c in range(2):
                mix = mix + jnp.dot(
                    comb[s, :, c * side : (c + 1) * side], slots[c, s].reshape(side, width),
                    preferred_element_type=F32,
                )
            mixed_ref[s] = (mix * scale).astype(BF16)
        else:
            sub = split // 2
            for q in range(split):
                piece = slots[q % 2, s].reshape(n_exp, chips // sub, sub, SLOTS, part)[:, :, q // 2]
                mix = jnp.dot(
                    comb[s], piece.reshape(n_exp * cols, part), preferred_element_type=F32
                )
                mixed_ref[s, :, q * part : (q + 1) * part] = (mix * scale).astype(BF16)

    for copy in started:
        copy.wait_send()


def shards(n_seq, n_exp, tokens, router, w_in, w_out):
    seqs, length, width = tokens.shape
    cols = router.shape[1]
    hidden = w_in.shape[2]
    experts = cols // SLOTS
    split = n_seq // experts
    chips = n_seq // 2
    rows = length // n_exp
    part = width // split
    stat_rows = -(-2 * seqs // 8) * 8
    lanes = -(-seqs * n_seq // 128) * 128
    dma = pltpu.SemaphoreType.DMA
    return pl.pallas_call(
        functools.partial(layer, n_seq, n_exp),
        out_shape=jax.ShapeDtypeStruct((seqs, rows, width), BF16),
        in_specs=[pl.BlockSpec(memory_space=pl.ANY)] * 4,
        out_specs=pl.BlockSpec(memory_space=pltpu.VMEM),
        scratch_shapes=[
            pltpu.VMEM((seqs, length, width), BF16),
            pltpu.VMEM((n_exp, width, cols), BF16),
            pltpu.VMEM((width, hidden), BF16),
            pltpu.VMEM((hidden, width), BF16),
            pltpu.VMEM((seqs, cols, width), BF16),
            pltpu.VMEM((n_seq, seqs, SLOTS, width), BF16),
            pltpu.VMEM((stat_rows, cols), F32),
            pltpu.VMEM((n_seq, stat_rows, cols), F32),
            pltpu.VMEM((cols, lanes), F32),
            pltpu.VMEM((seqs * SLOTS, width), BF16),
            pltpu.VMEM((split, seqs, SLOTS, part), BF16),
            pltpu.VMEM((split, seqs, SLOTS, part), BF16),
            pltpu.VMEM((2, seqs, n_exp, chips * SLOTS, part), BF16),
            pltpu.VMEM((seqs, rows, n_exp * cols), BF16),
            pltpu.VMEM((seqs, rows, 128), F32),
            pltpu.VMEM((n_exp * cols,) * 2 if split == 1 else (16, 128), BF16),
            dma((4,)),
            dma((n_exp,)), dma((n_exp,)), dma((n_exp,)), dma((n_exp,)),
            dma((seqs, n_seq)), dma((seqs, n_seq)), dma((n_seq,)), dma((n_seq,)),
            dma((split,)), dma((split,)),
            dma((n_exp,)), dma((n_exp,)),
            dma((n_exp, chips)), dma((n_exp, chips)),
            dma((n_exp,)), dma((n_exp,)),
        ],
        compiler_params=pltpu.CompilerParams(
            collective_id=0, has_side_effects=True, vmem_limit_bytes=56 * 1024 * 1024
        ),
    )(tokens, router, w_in, w_out)


def solution(mesh):
    placed = (
        P(None, "seq", None),
        P(None, "exp"),
        P(("exp", "seq"), None, None),
        P(("exp", "seq"), None, None),
    )
    return jax.shard_map(
        functools.partial(shards, mesh.shape["seq"], mesh.shape["exp"]),
        mesh=mesh, in_specs=placed, out_specs=P(None, ("seq", "exp"), None), check_vma=False,
    )
```
